256 devices in a mesh: grp: 8 (over z), cast: 8 (over y_lo, x), wid: 4 (over y_hi, core).
Axes of the slice: x: 4, y: 4 (y_hi: 2, y_lo: 2; y = y_hi * 2 + y_lo), z: 8, core: 2. Of those that a mesh axis runs over, the one named last changes fastest.
Arguments:
- fields: float32 [8, 4, 128, 128, 512], P('grp', None, None, 'cast', 'wid'), may hold values from -6 to 6
- velocity: float32 [8, 128, 128, 512], P('grp', None, 'cast', 'wid'), may hold values from 0.05 to 1
- liquid_mask: int32 [8, 16, 32], P('grp', 'cast', 'wid'), may hold values 0 or 1
- diffusion: float32 [8, 4], P('grp'), may hold values from 0.8 to 1.6
- port_cell: int32 [8, 8, 4, 256], P('grp', 'cast', 'wid'), may hold values from 258 to 1789, as said below
- handoff_count: int32 [8, 8, 4], P('grp', 'cast', 'wid'), may hold values from 1 to 256
Outputs:
- fields_out: float32 [8, 4, 128, 128, 512], P('grp', None, None, 'cast', 'wid')
The draws below stay inside these ranges and needn't reach their ends.
Inputs may be any that keep to these rules, and one draw needn't show every extreme that they name: `port_cell`: every named cell lies at least 2 cells from the rim of the device's block of 16 x 128 cells along both directions; cells may repeat.
All inputs are finite; a program needn't handle non-finite values. No bound on the sum of `liquid_mask` on one device may be relied on, other than what follows from the above.
Results may differ from the reference program's by a relative error of at most 0.00002.
Values sent between devices are 32-bit elements; how exact they have to be, the bound alone decides.
A program may use at most 128 MiB of HBM per device.

```python
import math
import jax
import jax.numpy as jnp

DEP = 128
CL = 16
CW = 128
PORT = 256
NL = 128
NW = 512
N_GRP = 8
N_CAST = 8
N_WID = 4


def draw_port_cell(key, part):
    key = jax.random.fold_in(key, 11)
    key_rows, key_cols = jax.random.split(key)
    shape_all = (N_GRP, N_CAST, N_WID, PORT)
    row_part = jax.random.randint(key_rows, shape_all, 2, CL - 2)
    col_part = jax.random.randint(key_cols, shape_all, 2, CW - 2)
    cells = row_part * CW + col_part
    cells = cells.at[..., 0].set(2 * CW + 2)
    cells = cells.at[..., 1].set((CL - 3) * CW + CW - 3)
    return cells.astype(jnp.int32)


def draw_handoff_count(key, part):
    key = jax.random.fold_in(key, 23)
    counts = jax.random.randint(key, (N_GRP, N_CAST, N_WID), 1, PORT + 1)
    counts = counts.at[0, 0, 0].set(PORT)
    counts = counts.at[N_GRP - 1, N_CAST - 1, N_WID - 1].set(1)
    return counts.astype(jnp.int32)


def with_ends(array, own_key, least, high):
    spot = [jax.random.randint(jax.random.fold_in(own_key, axis), (), 0, length) for axis, length in enumerate(array.shape)]
    widest = array.shape.index(max(array.shape))
    neighbour = spot[:widest] + [(spot[widest] + 1) % array.shape[widest]] + spot[widest + 1:]
    return array.at[tuple(spot)].set(least).at[tuple(neighbour)].set(high)


def levels(key, shape, cuts, least, high):
    level = 1.0
    for position, shards_of in cuts:
        heights = jax.random.uniform(jax.random.fold_in(jax.random.fold_in(key, 6), position), (shards_of,), jnp.float32, least / len(cuts), high / len(cuts))
        level = level * jnp.repeat(jnp.exp(heights), shape[position] // shards_of).reshape((-1,) + (1,) * (len(shape) - 1 - position))
    return level


def centred(own_key, shape, scale, most, cuts=(), held_as=jnp.bfloat16):
    drawn = jax.random.normal(own_key, shape, jnp.float32) * scale
    if len(cuts) > 0:
        drawn = levels(own_key, shape, cuts, -0.22, 0.18) * drawn
    return jnp.clip(drawn, min=-most, max=most).astype(held_as)


def setup_inputs(seed: int = 0) -> dict:
    arg_keys = jax.random.split(jax.random.key(seed), 7)
    return {
        "fields": centred(arg_keys[0], (N_GRP, 4, DEP, NL, NW), 1.0, 6.0, ((0, 8), (3, 8), (4, 4)), jnp.float32),
        "velocity": jnp.clip(jnp.exp(math.log(1.0) - 2.9957323 * jax.random.uniform(arg_keys[1], (N_GRP, DEP, NL, NW), jnp.float32) ** levels(arg_keys[1], (N_GRP, DEP, NL, NW), ((0, 8), (2, 8), (3, 4)), -0.2, 0.2)), 0.05, 1.0),
        "liquid_mask": with_ends((jax.random.randint(arg_keys[2], (N_GRP, NL // 8, NW // 16), 0, 4) < 3).astype(jnp.int32), jax.random.fold_in(arg_keys[2], 1), 0, 1),
        "diffusion": jnp.clip(jnp.exp(math.log(1.6) - 0.6931472 * jax.random.uniform(arg_keys[3], (N_GRP, 4), jnp.float32) ** levels(arg_keys[3], (N_GRP, 4), ((0, 8),), -0.2, 0.2)), 0.8, 1.6),
        "port_cell": draw_port_cell(jax.random.fold_in(arg_keys[6], 71), 0),
        "handoff_count": draw_handoff_count(jax.random.fold_in(arg_keys[6], 71), 0),
    }


STEP_SIZE = 0.1
RELAXATION = 0.5


def shifted(padded, offset):
    extent = padded.shape
    return padded[:, 2 + offset[0]:extent[1] - 2 + offset[0], 2 + offset[1]:extent[2] - 2 + offset[1], 2 + offset[2]:extent[3] - 2 + offset[2]]


def advance(extended, speed, liquid, diffusion_rates):
    padded = jnp.pad(extended, ((0, 0), (2, 2), (0, 0), (0, 0)))
    centre = shifted(padded, (0, 0, 0))
    laplace = -90.0 * centre
    for axis_number in range(3):
        for reach, weight in ((1, 16.0), (2, -1.0)):
            forward = [0, 0, 0]
            forward[axis_number] = reach
            backward = [0, 0, 0]
            backward[axis_number] = -reach
            laplace = laplace + weight * (shifted(padded, forward) + shifted(padded, backward))
    laplace = laplace / 12.0
    upwind = centre - shifted(padded, (0, -1, 0))
    return centre + STEP_SIZE * (liquid[None] * diffusion_rates[:, None, None, None] * laplace - speed[None] * upwind)


def reference(fields, velocity, liquid_mask, diffusion, port_cell, handoff_count):
    half_groups = N_GRP // 2
    total_rows = CL * N_CAST
    total_cols = CW * N_WID
    liquid = 0.25 + 0.75 * jnp.repeat(jnp.repeat(liquid_mask.astype(jnp.float32), 8, axis=1), 16, axis=2)
    cast_start = (jnp.arange(N_CAST, dtype=jnp.int32) * CL)[None, :, None, None]
    wid_start = (jnp.arange(N_WID, dtype=jnp.int32) * CW)[None, None, :, None]
    row_index = cast_start + port_cell // CW
    col_index = wid_start + port_cell % CW
    flat_index = (row_index * total_cols + col_index).astype(jnp.int32).reshape(N_GRP, -1)
    active = (jnp.arange(PORT, dtype=jnp.int32)[None, None, None, :] < handoff_count[..., None]).astype(jnp.float32).reshape(N_GRP, -1)
    current = [fields[group] for group in range(N_GRP)]
    for step_index in range(2):
        outgoing = []
        for group in range(N_GRP):
            layer_index = DEP - 1 if group < half_groups else 0
            outgoing.append(current[group][:, layer_index].reshape(4, -1)[:, flat_index[group]])
        updated = []
        for group in range(N_GRP):
            layer_index = DEP - 1 if group < half_groups else 0
            extended = jnp.pad(current[group], ((0, 0), (0, 0), (2, 2), (2, 2)))
            fresh = advance(extended, velocity[group], liquid[group], diffusion[group])
            surface = fresh[:, layer_index].reshape(4, -1)
            received = outgoing[(group + half_groups) % N_GRP]
            change = RELAXATION * (received - surface[:, flat_index[group]]) * active[group][None]
            surface = surface.at[:, flat_index[group]].add(change)
            fresh = fresh.at[:, layer_index].set(surface.reshape(4, total_rows, total_cols))
            updated.append(fresh)
        current = updated
    return jnp.stack(current)
```

```python
import functools

import jax
import jax.numpy as jnp
from jax import lax
from jax.experimental import pallas as pl
from jax.experimental.pallas import tpu as pltpu
from jax.sharding import PartitionSpec as P

STEP_SIZE = 0.1
RELAXATION = 0.5
COMPS = 4
CHUNK = 8
SIDE_ROWS = 8
MESH = pl.DeviceIdType.MESH
EXACT = lax.Precision.HIGHEST


def kernel(
    fields,
    velocity,
    mask,
    diffusion,
    cells,
    count,
    out,
    first,
    second,
    result,
    speed,
    rate,
    packed,
    from_left,
    from_right,
    onehot,
    live,
    layer,
    hits,
    outgoing,
    received,
    load_sem,
    speed_sem,
    store_sem,
    cast_send,
    cast_recv,
    wid_send,
    wid_recv,
    port_send,
    port_recv,
):
    depth, rows, cols = fields.shape[2:]
    ports = cells.shape[-1]
    chunks = depth // CHUNK
    tiles = rows // 8
    below = SIDE_ROWS + rows
    grp, cast, wid = (lax.axis_index(name) for name in ("grp", "cast", "wid"))
    n_grp, n_cast, n_wid = (lax.axis_size(name) for name in ("grp", "cast", "wid"))
    other = lax.rem(grp + n_grp // 2, n_grp)
    tundish = (grp < n_grp // 2).astype(jnp.int32)
    surface = tundish * (depth - 1)
    has_up, has_down = cast > 0, cast < n_cast - 1
    has_left, has_right = wid > 0, wid < n_wid - 1
    sides = (
        (has_up, {"cast": cast - 1}),
        (has_down, {"cast": cast + 1}),
        (has_left, {"wid": wid - 1}),
        (has_right, {"wid": wid + 1}),
    )

    def place(index):
        return index + tundish * (chunks - 1 - 2 * index)

    def load(chunk):
        at = pl.ds(chunk * CHUNK, CHUNK)
        return pltpu.make_async_copy(
            fields.at[0, :, at],
            first.at[:, pl.ds(2 + chunk * CHUNK, CHUNK), pl.ds(SIDE_ROWS, rows)],
            load_sem.at[chunk],
        )

    load_speed = pltpu.make_async_copy(velocity.at[0], speed, speed_sem)
    for_all = functools.partial(lax.fori_loop, 0, chunks)

    def start_load(index, carry):
        load(place(index)).start()
        return carry

    for_all(start_load, 0)
    load_speed.start()

    barrier = pltpu.get_barrier_semaphore()
    for there, device in sides:

        @pl.when(there)
        def _():
            pl.semaphore_signal(barrier, 1, device_id=device, device_id_type=MESH)

    pl.semaphore_signal(barrier, 1, device_id={"grp": other}, device_id_type=MESH)
    neighbours = 1
    for there, _ in sides:
        neighbours = neighbours + there.astype(jnp.int32)
    pl.semaphore_wait(barrier, neighbours)

    def cast_copy(step, chunk, down):
        own = (rows - 2 if down else 0) + (SIDE_ROWS if step else 0)
        at = pl.ds(2 + chunk * CHUNK, CHUNK)
        if step:
            source = second.at[:, at, pl.ds(own, 2)]
            target = second
        else:
            source = fields.at[0, :, pl.ds(chunk * CHUNK, CHUNK), pl.ds(own, 2)]
            target = first
        return pltpu.make_async_remote_copy(
            src_ref=source,
            dst_ref=target.at[:, at, pl.ds(SIDE_ROWS - 2 if down else below, 2)],
            send_sem=cast_send.at[step, down, chunk],
            recv_sem=cast_recv.at[step, down, chunk],
            device_id={"cast": cast + 1 if down else cast - 1},
            device_id_type=MESH,
        )

    def wid_copy(step, chunk, right):
        target = from_left if right else from_right
        return pltpu.make_async_remote_copy(
            src_ref=packed.at[step, chunk],
            dst_ref=target.at[step, chunk],
            send_sem=wid_send.at[step, right, chunk],
            recv_sem=wid_recv.at[step, right, chunk],
            device_id={"wid": wid + 1 if right else wid - 1},
            device_id_type=MESH,
        )

    def port_copy(step):
        return pltpu.make_async_remote_copy(
            src_ref=outgoing.at[step],
            dst_ref=received.at[step],
            send_sem=port_send.at[step],
            recv_sem=port_recv.at[step],
            device_id={"grp": other},
            device_id_type=MESH,
        )

    def send(copy, step, chunk):
        there = (has_up, has_down) if copy is cast_copy else (has_left, has_right)
        for way in range(2):

            @pl.when(there[way])
            def _():
                copy(step, chunk, way).start()

    def arrive(copy, step, chunk):
        there = (has_down, has_up) if copy is cast_copy else (has_right, has_left)
        for way in range(2):

            @pl.when(there[way])
            def _():
                copy(step, chunk, way).wait_recv()

    def sent(copy, step, chunk):
        there = (has_up, has_down) if copy is cast_copy else (has_left, has_right)
        for way in range(2):

            @pl.when(there[way])
            def _():
                copy(step, chunk, way).wait_send()

    def send_first(index, carry):
        send(cast_copy, 0, place(index))
        return carry

    for_all(send_first, 0)

    for ref in (first, second):
        for comp in range(COMPS):
            for at in (0, 1, depth + 2, depth + 3):
                ref[comp, at, SIDE_ROWS:below] = jnp.zeros((rows, cols), jnp.float32)

    for there, start in ((has_up, SIDE_ROWS - 2), (has_down, below)):

        @pl.when(jnp.logical_not(there))
        def _():
            @pl.loop(0, depth)
            def _(at):
                for ref in (first, second):
                    for comp in range(COMPS):
                        ref[comp, at + 2, start : start + 2] = jnp.zeros((2, cols), jnp.float32)

    for there, ref in ((has_left, from_left), (has_right, from_right)):

        @pl.when(jnp.logical_not(there))
        def _():
            ref[...] = jnp.zeros(ref.shape, jnp.float32)

    lane = lax.broadcasted_iota(jnp.int32, (8, cols), 1)
    slot_lane = lane // 4

    for tile in range(tiles):
        liquid = jnp.zeros((8, cols), jnp.float32)
        for block in range(mask.shape[2]):
            value = 0.25 + 0.75 * mask[0, tile, block].astype(jnp.float32)
            liquid = jnp.where(lane // 16 == block, value, liquid)
        for comp in range(COMPS):
            rate[comp, tile * 8 : tile * 8 + 8] = liquid * (diffusion[0, comp] * (STEP_SIZE / 12.0))

    cell = cells[0, 0]
    cell_row, cell_col = cell // cols, lax.rem(cell, cols)
    onehot[...] = (lax.broadcasted_iota(jnp.int32, (cols, ports), 0) == cell_col).astype(jnp.float32)
    row_hot = (lax.broadcasted_iota(jnp.int32, (rows, ports), 0) == cell_row).astype(jnp.float32)
    active = (lax.broadcasted_iota(jnp.int32, (1, ports), 1) < count[0, 0, 0]).astype(jnp.float32)
    live[0] = row_hot
    live[1] = row_hot * active
    hits[...] = lax.dot_general(
        live[1],
        onehot[...],
        (((1,), (1,)), ((), ())),
        precision=EXACT,
        preferred_element_type=jnp.float32,
    )

    def gather(step, ref):
        flat = jnp.concatenate(
            [ref[comp, 2 + surface, SIDE_ROWS:below] for comp in range(COMPS)], axis=0
        )
        wide = jnp.dot(flat, onehot[...], precision=EXACT, preferred_element_type=jnp.float32)
        for comp in range(COMPS):
            picked = wide[comp * rows : comp * rows + rows] * live[0]
            outgoing[step, comp : comp + 1] = jnp.sum(picked, axis=0, keepdims=True)

    def scatter(step):
        flat = jnp.concatenate(
            [live[1] * received[step, comp : comp + 1] for comp in range(COMPS)], axis=0
        )
        layer[...] = lax.dot_general(
            flat,
            onehot[...],
            (((1,), (1,)), ((), ())),
            precision=EXACT,
            preferred_element_type=jnp.float32,
        )

    def pack(tile_value, slot, total):
        turned = pltpu.roll(tile_value, 4 * slot + 2, 1)
        return jnp.where(slot_lane == slot, turned, total)

    def pack_first(index, carry):
        chunk = place(index)
        load(chunk).wait()
        for tile in range(tiles):
            total = jnp.zeros((8, cols), jnp.float32)
            for comp in range(COMPS):
                for at in range(CHUNK):
                    value = first[comp, 2 + chunk * CHUNK + at, pl.ds(SIDE_ROWS + tile * 8, 8)]
                    total = pack(value, comp * CHUNK + at, total)
            packed[0, chunk, tile * 8 : tile * 8 + 8] = total
        send(wid_copy, 0, chunk)
        return carry

    for_all(pack_first, 0)
    gather(0, first)
    port_copy(0).start()

    load_speed.wait()

    def advance(step, chunk):
        source = second if step else first
        base = chunk * CHUNK
        for tile in range(tiles):
            at_row = SIDE_ROWS + tile * 8
            own = pl.ds(tile * 8, 8)
            edge = jnp.where(
                lax.rem(lane, 4) < 2,
                from_left[step, chunk, own],
                from_right[step, chunk, own],
            )
            total = jnp.zeros((8, cols), jnp.float32)
            for comp in range(COMPS):
                factor = rate[comp, own]
                column = [
                    source[comp, base + at, pl.ds(at_row, 8)] for at in range(CHUNK + 4)
                ]
                for at in range(CHUNK):
                    slot = comp * CHUNK + at
                    here = base + 2 + at
                    value = column[at + 2]
                    up1, up2, down1, down2 = (
                        source[comp, here, pl.ds(at_row + shift, 8)] for shift in (-1, -2, 1, 2)
                    )
                    side = pltpu.roll(edge, (cols - 4 * slot - 2) % cols, 1)
                    left1 = pltpu.roll(jnp.where(lane == cols - 1, side, value), 1, 1)
                    left2 = pltpu.roll(jnp.where(lane >= cols - 2, side, value), 2, 1)
                    right1 = pltpu.roll(jnp.where(lane == 0, side, value), cols - 1, 1)
                    right2 = pltpu.roll(jnp.where(lane < 2, side, value), cols - 2, 1)
                    near = (up1 + down1) + (left1 + right1) + (column[at + 1] + column[at + 3])
                    far = (up2 + down2) + (left2 + right2) + (column[at] + column[at + 4])
                    laplace = (16.0 * near - far) - 90.0 * value
                    flow = (STEP_SIZE * speed[base + at, own]) * (value - up1)
                    fresh = value + (factor * laplace - flow)
                    if step:
                        result[comp, base + at, own] = fresh
                    else:
                        second[comp, here, pl.ds(at_row, 8)] = fresh
                        total = pack(fresh, slot, total)
            if not step:
                packed[1, chunk, own] = total

    def step_one(index, carry):
        chunk = place(index)
        arrive(wid_copy, 0, chunk)
        arrive(cast_copy, 0, chunk)
        advance(0, chunk)
        send(cast_copy, 1, chunk)
        send(wid_copy, 1, chunk)
        return carry

    for_all(step_one, 0)

    port_copy(0).wait_recv()
    scatter(0)
    inner = pl.ds(SIDE_ROWS + 2, rows - 4)
    for comp in range(COMPS):
        old = second[comp, 2 + surface, inner]
        change = layer[comp * rows + 2 : comp * rows + rows - 2] - hits[2 : rows - 2] * old
        second[comp, 2 + surface, inner] = old + RELAXATION * change
    gather(1, second)
    port_copy(1).start()

    def store(chunk):
        at = pl.ds(chunk * CHUNK, CHUNK)
        return pltpu.make_async_copy(result.at[:, at], out.at[0, :, at], store_sem.at[chunk])

    def step_two(index, carry):
        chunk = place(index)
        arrive(wid_copy, 1, chunk)
        arrive(cast_copy, 1, chunk)
        advance(1, chunk)

        @pl.when(index > 0)
        def _():
            store(chunk).start()

        return carry

    for_all(step_two, 0)

    port_copy(1).wait_recv()
    scatter(1)
    for comp in range(COMPS):
        old = result[comp, surface]
        change = layer[comp * rows : comp * rows + rows] - hits[...] * old
        result[comp, surface] = old + RELAXATION * change
    store(place(0)).start()

    def finish(index, carry):
        chunk = place(index)
        for step in range(2):
            sent(cast_copy, step, chunk)
            sent(wid_copy, step, chunk)
        store(chunk).wait()
        return carry

    for_all(finish, 0)
    for step in range(2):
        port_copy(step).wait_send()


def per_device(fields, velocity, liquid_mask, diffusion, port_cell, handoff_count):
    _, comps, depth, rows, cols = fields.shape
    ports = port_cell.shape[-1]
    chunks = depth // CHUNK
    f32 = jnp.float32
    padded = pltpu.VMEM((comps, depth + 4, rows + 2 * SIDE_ROWS, cols), f32)
    strips = pltpu.VMEM((2, chunks, rows, cols), f32)
    dma = pltpu.SemaphoreType.DMA
    anywhere = pl.BlockSpec(memory_space=pl.ANY)
    smem = pl.BlockSpec(memory_space=pltpu.SMEM)
    return pl.pallas_call(
        kernel,
        out_shape=jax.ShapeDtypeStruct(fields.shape, f32),
        in_specs=[anywhere, anywhere, smem, smem, pl.BlockSpec(memory_space=pltpu.VMEM), smem],
        out_specs=anywhere,
        scratch_shapes=[
            padded,
            padded,
            pltpu.VMEM((comps, depth, rows, cols), f32),
            pltpu.VMEM((depth, rows, cols), f32),
            pltpu.VMEM((comps, rows, cols), f32),
            strips,
            strips,
            strips,
            pltpu.VMEM((cols, ports), f32),
            pltpu.VMEM((2, rows, ports), f32),
            pltpu.VMEM((comps * rows, cols), f32),
            pltpu.VMEM((rows, cols), f32),
            pltpu.VMEM((2, comps, ports), f32),
            pltpu.VMEM((2, comps, ports), f32),
            dma((chunks,)),
            dma,
            dma((chunks,)),
            dma((2, 2, chunks)),
            dma((2, 2, chunks)),
            dma((2, 2, chunks)),
            dma((2, 2, chunks)),
            dma((2,)),
            dma((2,)),
        ],
        compiler_params=pltpu.CompilerParams(
            collective_id=0, has_side_effects=True, vmem_limit_bytes=48 * 2**20
        ),
        cost_estimate=pl.CostEstimate(
            flops=60 * fields.size, bytes_accessed=9 * 2**20, transcendentals=0
        ),
    )(fields, velocity, liquid_mask, diffusion, port_cell, handoff_count)


def solution(mesh):
    in_specs = (
        P("grp", None, None, "cast", "wid"),
        P("grp", None, "cast", "wid"),
        P("grp", "cast", "wid"),
        P("grp", None),
        P("grp", "cast", "wid", None),
        P("grp", "cast", "wid"),
    )
    out_specs = P("grp", None, None, "cast", "wid")
    return jax.shard_map(
        per_device, mesh=mesh, in_specs=in_specs, out_specs=out_specs, check_vma=False
    )
```

```python
import functools

import jax
import jax.numpy as jnp
from jax import lax
from jax.experimental import pallas as pl
from jax.experimental.pallas import tpu as pltpu
from jax.sharding import PartitionSpec as P

STEP_SIZE = 0.1
RELAXATION = 0.5
COMPS = 4
CHUNK = 8
SIDE_ROWS = 8
MESH = pl.DeviceIdType.MESH
EXACT = lax.Precision.HIGHEST


def kernel(
    fields,
    velocity,
    mask_at,
    diffusion_at,
    cells_at,
    count_at,
    out,
    first,
    second,
    speed,
    mask,
    diffusion,
    cells,
    count,
    rate,
    band,
    packed,
    from_left,
    from_right,
    onehot,
    live,
    layer,
    hits,
    outgoing,
    received,
    load_sem,
    speed_sem,
    small_sem,
    cast_send,
    cast_recv,
    wid_send,
    wid_recv,
    port_send,
    port_recv,
    word_sem,
):
    depth, rows, cols = fields.shape[2:]
    ports = cells.shape[-1]
    chunks = depth // CHUNK
    result = out.at[0]
    tiles = rows // 8
    below = SIDE_ROWS + rows
    grp, cast, wid = (lax.axis_index(name) for name in ("grp", "cast", "wid"))
    n_grp, n_cast, n_wid = (lax.axis_size(name) for name in ("grp", "cast", "wid"))
    other = lax.rem(grp + n_grp // 2, n_grp)
    tundish = (grp < n_grp // 2).astype(jnp.int32)
    surface = tundish * (depth - 1)
    has_up, has_down = cast > 0, cast < n_cast - 1
    has_left, has_right = wid > 0, wid < n_wid - 1
    sides = (
        (has_up, {"cast": cast - 1}),
        (has_down, {"cast": cast + 1}),
        (has_left, {"wid": wid - 1}),
        (has_right, {"wid": wid + 1}),
    )

    barrier = pltpu.get_barrier_semaphore()
    for there, device in sides:

        @pl.when(there)
        def _():
            pl.semaphore_signal(barrier, 1, device_id=device, device_id_type=MESH)

    previous = {"grp": lax.rem(grp + n_grp - 1, n_grp)}
    following = {"grp": lax.rem(grp + 1, n_grp)}
    pl.semaphore_signal(barrier, 1, device_id=previous, device_id_type=MESH)

    def place(index):
        return index + tundish * (chunks - 1 - 2 * index)

    def load(chunk):
        at = pl.ds(chunk * CHUNK, CHUNK)
        return pltpu.make_async_copy(
            fields.at[0, :, at],
            first.at[:, pl.ds(2 + chunk * CHUNK, CHUNK), pl.ds(SIDE_ROWS, rows)],
            load_sem.at[chunk],
        )

    load_speed = pltpu.make_async_copy(velocity.at[0], speed, speed_sem)
    for_all = functools.partial(lax.fori_loop, 0, chunks)

    def start_load(index, carry):
        load(place(index)).start()
        return carry

    small = [
        pltpu.make_async_copy(source, target, small_sem.at[index])
        for index, (source, target) in enumerate(
            ((mask_at, mask), (diffusion_at, diffusion), (cells_at, cells), (count_at, count))
        )
    ]
    for_all(start_load, 0)
    for copy in small:
        copy.start()
    load_speed.start()

    neighbours = 1
    for there, _ in sides:
        neighbours = neighbours + there.astype(jnp.int32)
    pl.semaphore_wait(barrier, neighbours)

    def pass_word(hop):
        pl.semaphore_signal(word_sem.at[hop], 1, device_id=following, device_id_type=MESH)

    pass_word(0)

    def cast_copy(step, chunk, down):
        own = (rows - 2 if down else 0) + (SIDE_ROWS if step else 0)
        start, size = (0, depth) if chunk is None else (chunk * CHUNK, CHUNK)
        at = pl.ds(2 + start, size)
        if step:
            source = second.at[:, at, pl.ds(own, 2)]
            target = second
        else:
            source = fields.at[0, :, pl.ds(start, size), pl.ds(own, 2)]
            target = first
        return pltpu.make_async_remote_copy(
            src_ref=source,
            dst_ref=target.at[:, at, pl.ds(SIDE_ROWS - 2 if down else below, 2)],
            send_sem=cast_send.at[step, down],
            recv_sem=cast_recv.at[step, down, 0 if chunk is None else chunk],
            device_id={"cast": cast + 1 if down else cast - 1},
            device_id_type=MESH,
        )

    def wid_copy(step, chunk, right):
        target = from_left if right else from_right
        at = pl.ds(0, chunks) if chunk is None else chunk
        return pltpu.make_async_remote_copy(
            src_ref=packed.at[step, at],
            dst_ref=target.at[step, at],
            send_sem=wid_send.at[step, right],
            recv_sem=wid_recv.at[step, right, 0 if chunk is None else chunk],
            device_id={"wid": wid + 1 if right else wid - 1},
            device_id_type=MESH,
        )

    def port_copy(step):
        return pltpu.make_async_remote_copy(
            src_ref=outgoing.at[step],
            dst_ref=received.at[step],
            send_sem=port_send.at[step],
            recv_sem=port_recv.at[step],
            device_id={"grp": other},
            device_id_type=MESH,
        )

    def send(copy, step, chunk):
        there = (has_up, has_down) if copy is cast_copy else (has_left, has_right)
        for way in range(2):

            @pl.when(there[way])
            def _():
                copy(step, chunk, way).start()

    def arrive(copy, step, chunk):
        there = (has_down, has_up) if copy is cast_copy else (has_right, has_left)
        for way in range(2):

            @pl.when(there[way])
            def _():
                copy(step, chunk, way).wait_recv()

    def sent(copy, step):
        there = (has_up, has_down) if copy is cast_copy else (has_left, has_right)
        for way in range(2):

            @pl.when(there[way])
            def _():
                copy(step, None, way).wait_send()

    def send_first(index, carry):
        send(cast_copy, 0, place(index))
        return carry

    for_all(send_first, 0)

    lane = lax.broadcasted_iota(jnp.int32, (8, cols), 1)
    slot_lane = lane // 4

    def pack(tile_value, slot, total):
        turned = pltpu.roll(tile_value, 4 * slot + 2, 1)
        return jnp.where(slot_lane == slot, turned, total)

    def pack_first(index, carry):
        chunk = place(index)
        load(chunk).wait()
        for tile in range(tiles):
            total = jnp.zeros((8, cols), jnp.float32)
            for comp in range(COMPS):
                for at in range(CHUNK):
                    value = first[comp, 2 + chunk * CHUNK + at, pl.ds(SIDE_ROWS + tile * 8, 8)]
                    total = pack(value, comp * CHUNK + at, total)
            packed[0, chunk, tile * 8 : tile * 8 + 8] = total
        send(wid_copy, 0, chunk)
        return carry

    for_all(pack_first, 0)
    for ref in (first, second):
        for comp in range(COMPS):
            for at in (0, 1, depth + 2, depth + 3):
                ref[comp, at, SIDE_ROWS:below] = jnp.zeros((rows, cols), jnp.float32)

    for there, start in ((has_up, SIDE_ROWS - 2), (has_down, below)):

        @pl.when(jnp.logical_not(there))
        def _():
            @pl.loop(0, depth)
            def _(at):
                for ref in (first, second):
                    for comp in range(COMPS):
                        ref[comp, at + 2, start : start + 2] = jnp.zeros((2, cols), jnp.float32)

    for there, ref in ((has_left, from_left), (has_right, from_right)):

        @pl.when(jnp.logical_not(there))
        def _():
            ref[...] = jnp.zeros(ref.shape, jnp.float32)

    down, across = (lax.broadcasted_iota(jnp.int32, (2 * cols, cols), axis) for axis in (0, 1))
    apart = jnp.abs((down & (cols - 1)) - across)
    weight = jnp.where(apart == 1, 16.0, jnp.where(apart == 2, -1.0, 0.0))
    band[...] = weight.astype(jnp.bfloat16)

    for copy in small:
        copy.wait()

    for tile in range(tiles):
        liquid = jnp.zeros((8, cols), jnp.float32)
        for block in range(mask.shape[2]):
            value = 0.25 + 0.75 * mask[0, tile, block].astype(jnp.float32)
            liquid = jnp.where(lane // 16 == block, value, liquid)
        for comp in range(COMPS):
            rate[comp, tile * 8 : tile * 8 + 8] = liquid * (diffusion[0, comp] * (STEP_SIZE / 12.0))

    cell = cells[0, 0]
    cell_row, cell_col = cell >> (cols.bit_length() - 1), cell & (cols - 1)
    onehot[...] = (lax.broadcasted_iota(jnp.int32, (cols, ports), 0) == cell_col).astype(jnp.float32)
    row_hot = (lax.broadcasted_iota(jnp.int32, (rows, ports), 0) == cell_row).astype(jnp.float32)
    active = (lax.broadcasted_iota(jnp.int32, (1, ports), 1) < count[0, 0, 0]).astype(jnp.float32)
    live[0] = row_hot
    live[1] = row_hot * active
    hits[...] = lax.dot_general(
        live[1],
        onehot[...],
        (((1,), (1,)), ((), ())),
        precision=EXACT,
        preferred_element_type=jnp.float32,
    )

    def gather(step, ref):
        flat = jnp.concatenate(
            [ref[comp, 2 + surface, SIDE_ROWS:below] for comp in range(COMPS)], axis=0
        )
        wide = jnp.dot(flat, onehot[...], precision=EXACT, preferred_element_type=jnp.float32)
        for comp in range(COMPS):
            picked = wide[comp * rows : comp * rows + rows] * live[0]
            outgoing[step, comp : comp + 1] = jnp.sum(picked, axis=0, keepdims=True)

    def scatter(step):
        flat = jnp.concatenate(
            [live[1] * received[step, comp : comp + 1] for comp in range(COMPS)], axis=0
        )
        layer[...] = lax.dot_general(
            flat,
            onehot[...],
            (((1,), (1,)), ((), ())),
            precision=EXACT,
            preferred_element_type=jnp.float32,
        )

    gather(0, first)

    load_speed.wait()

    def scale(at, carry):
        speed[at] = STEP_SIZE * speed[at]
        return carry

    lax.fori_loop(0, depth, scale, 0, unroll=8)

    def rim_terms(step, chunk, own):
        place_in_slot = lane & 3
        edge = jnp.where(
            place_in_slot < 2, from_left[step, chunk, own], from_right[step, chunk, own]
        )
        after1, after2, before1, before2 = (
            pltpu.roll(edge, shift, 1) for shift in (cols - 1, cols - 2, 1, 2)
        )
        near = jnp.where(place_in_slot == 1, after1, jnp.where(place_in_slot == 2, before1, 0.0))
        return 16.0 * near - jnp.where(place_in_slot < 2, after2, before2)

    at_rim = (lane < 2) | (lane >= cols - 2)

    def advance(step, chunk):
        source = second if step else first
        base = chunk * CHUNK
        owns = [pl.ds(tile * 8, 8) for tile in range(tiles)]
        rims = [rim_terms(step, chunk, own) for own in owns]
        totals = [jnp.zeros((8, cols), jnp.float32) for _ in owns]
        for comp in range(COMPS):
            block = source[comp, pl.ds(base + 2, CHUNK), pl.ds(SIDE_ROWS, rows)]
            block = block.reshape(CHUNK * rows, cols)
            high = block.astype(jnp.bfloat16)
            low = (block - high.astype(jnp.float32)).astype(jnp.bfloat16)
            width = jnp.dot(
                jnp.concatenate([high, low], axis=1),
                band[...],
                preferred_element_type=jnp.float32,
            )
            for tile, own in enumerate(owns):
                at_row = SIDE_ROWS + tile * 8
                factor = rate[comp, own]
                column = [
                    source[comp, base + at, pl.ds(at_row, 8)] for at in range(CHUNK + 4)
                ]
                for at in range(CHUNK):
                    slot = comp * CHUNK + at
                    here = base + 2 + at
                    value = column[at + 2]
                    up1, up2, down1, down2 = (
                        source[comp, here, pl.ds(at_row + shift, 8)] for shift in (-1, -2, 1, 2)
                    )
                    side = pltpu.roll(rims[tile], (cols - 4 * slot - 2) % cols, 1)
                    start = at * rows + tile * 8
                    sideways = width[start : start + 8] + jnp.where(at_rim, side, 0.0)
                    near = (up1 + down1) + (column[at + 1] + column[at + 3])
                    far = (up2 + down2) + (column[at] + column[at + 4])
                    laplace = (16.0 * near - far) + (sideways - 90.0 * value)
                    flow = speed[base + at, own] * (value - up1)
                    fresh = value + (factor * laplace - flow)
                    if step:
                        result[comp, base + at, own] = fresh
                    else:
                        second[comp, here, pl.ds(at_row, 8)] = fresh
                        totals[tile] = pack(fresh, slot, totals[tile])
        if not step:
            for own, total in zip(owns, totals):
                packed[1, chunk, own] = total

    def step_one(index, carry):
        chunk = place(index)
        arrive(wid_copy, 0, chunk)
        arrive(cast_copy, 0, chunk)
        advance(0, chunk)
        send(cast_copy, 1, chunk)
        send(wid_copy, 1, chunk)
        for hop in range(n_grp // 2):

            @pl.when(index == 2 * hop + 1)
            def _():
                pl.semaphore_wait(word_sem.at[hop], 1)
                if hop + 1 < n_grp // 2:
                    pass_word(hop + 1)
                else:
                    port_copy(0).start()

        return carry

    for_all(step_one, 0)

    port_copy(0).wait_recv()
    scatter(0)
    inner = pl.ds(SIDE_ROWS + 2, rows - 4)
    for comp in range(COMPS):
        old = second[comp, 2 + surface, inner]
        change = layer[comp * rows + 2 : comp * rows + rows - 2] - hits[2 : rows - 2] * old
        second[comp, 2 + surface, inner] = old + RELAXATION * change
    gather(1, second)
    port_copy(1).start()

    def step_two(index, carry):
        chunk = place(index)
        arrive(wid_copy, 1, chunk)
        arrive(cast_copy, 1, chunk)
        advance(1, chunk)
        return carry

    for_all(step_two, 0)

    port_copy(1).wait_recv()
    scatter(1)
    for comp in range(COMPS):
        old = result[comp, surface]
        change = layer[comp * rows : comp * rows + rows] - hits[...] * old
        result[comp, surface] = old + RELAXATION * change

    for step in range(2):
        sent(cast_copy, step)
        sent(wid_copy, step)
    for step in range(2):
        port_copy(step).wait_send()


def per_device(fields, velocity, liquid_mask, diffusion, port_cell, handoff_count):
    _, comps, depth, rows, cols = fields.shape
    ports = port_cell.shape[-1]
    chunks = depth // CHUNK
    f32 = jnp.float32
    padded = pltpu.VMEM((comps, depth + 4, rows + 2 * SIDE_ROWS, cols), f32)
    strips = pltpu.VMEM((2, chunks, rows, cols), f32)
    dma = pltpu.SemaphoreType.DMA
    return pl.pallas_call(
        kernel,
        out_shape=pltpu.VMEM(fields.shape, f32),
        in_specs=[pl.BlockSpec(memory_space=pltpu.HBM)] * 6,
        out_specs=pl.BlockSpec(memory_space=pltpu.VMEM),
        scratch_shapes=[
            padded,
            padded,
            pltpu.VMEM((depth, rows, cols), f32),
            pltpu.SMEM(liquid_mask.shape, jnp.int32),
            pltpu.SMEM(diffusion.shape, f32),
            pltpu.VMEM(port_cell.shape, jnp.int32),
            pltpu.SMEM(handoff_count.shape, jnp.int32),
            pltpu.VMEM((comps, rows, cols), f32),
            pltpu.VMEM((2 * cols, cols), jnp.bfloat16),
            strips,
            strips,
            strips,
            pltpu.VMEM((cols, ports), f32),
            pltpu.VMEM((2, rows, ports), f32),
            pltpu.VMEM((comps * rows, cols), f32),
            pltpu.VMEM((rows, cols), f32),
            pltpu.VMEM((2, comps, ports), f32),
            pltpu.VMEM((2, comps, ports), f32),
            dma((chunks,)),
            dma,
            dma((4,)),
            dma((2, 2)),
            dma((2, 2, chunks)),
            dma((2, 2)),
            dma((2, 2, chunks)),
            dma((2,)),
            dma((2,)),
            pltpu.SemaphoreType.REGULAR((lax.axis_size("grp") // 2,)),
        ],
        compiler_params=pltpu.CompilerParams(
            collective_id=0, has_side_effects=True, vmem_limit_bytes=54 * 2**20
        ),
        cost_estimate=pl.CostEstimate(
            flops=60 * fields.size, bytes_accessed=9 * 2**20, transcendentals=0
        ),
    )(fields, velocity, liquid_mask, diffusion, port_cell, handoff_count)


def solution(mesh):
    in_specs = (
        P("grp", None, None, "cast", "wid"),
        P("grp", None, "cast", "wid"),
        P("grp", "cast", "wid"),
        P("grp", None),
        P("grp", "cast", "wid", None),
        P("grp", "cast", "wid"),
    )
    out_specs = P("grp", None, None, "cast", "wid")
    return jax.shard_map(
        per_device, mesh=mesh, in_specs=in_specs, out_specs=out_specs, check_vma=False
    )
```

```python
import functools

import jax
import jax.numpy as jnp
from jax import lax
from jax.experimental import pallas as pl
from jax.experimental.pallas import tpu as pltpu
from jax.sharding import PartitionSpec as P

STEP_SIZE = 0.1
RELAXATION = 0.5
COMPS = 4
CHUNK = 8
SIDE_ROWS = 8
MESH = pl.DeviceIdType.MESH
EXACT = lax.Precision.HIGHEST


def kernel(
    fields,
    velocity,
    mask_at,
    diffusion_at,
    cells_at,
    count_at,
    out,
    first,
    second,
    speed,
    mask,
    diffusion,
    cells,
    count,
    rate,
    band,
    packed,
    from_left,
    from_right,
    onehot,
    live,
    layer,
    hits,
    outgoing,
    received,
    relayed,
    load_sem,
    speed_sem,
    small_sem,
    cast_send,
    cast_recv,
    wid_send,
    wid_recv,
    port_send,
    port_recv,
    word_sem,
    there_send,
    there_recv,
    on_send,
    on_recv,
):
    depth, rows, cols = fields.shape[2:]
    ports = cells.shape[-1]
    chunks = depth // CHUNK
    result = out.at[0]
    tiles = rows // 8
    below = SIDE_ROWS + rows
    grp, cast, wid = (lax.axis_index(name) for name in ("grp", "cast", "wid"))
    n_grp, n_cast, n_wid = (lax.axis_size(name) for name in ("grp", "cast", "wid"))
    other = lax.rem(grp + n_grp // 2, n_grp)
    tundish = (grp < n_grp // 2).astype(jnp.int32)
    surface = tundish * (depth - 1)
    has_up, has_down = cast > 0, cast < n_cast - 1
    has_left, has_right = wid > 0, wid < n_wid - 1
    sides = (
        (has_up, {"cast": cast - 1}),
        (has_down, {"cast": cast + 1}),
        (has_left, {"wid": wid - 1}),
        (has_right, {"wid": wid + 1}),
    )

    barrier = pltpu.get_barrier_semaphore()
    for there, device in sides:

        @pl.when(there)
        def _():
            pl.semaphore_signal(barrier, 1, device_id=device, device_id_type=MESH)

    middle = n_cast // 2
    above, below_middle = cast == middle - 1, cast == middle
    relay_down, relay_up = (n_cast - 1, 0)
    bends = (
        (above, relay_down),
        (below_middle, relay_up),
        (cast == relay_down, middle),
        (cast == relay_up, middle - 1),
    )
    greeted = (
        (above, relay_up),
        (below_middle, relay_down),
        (cast == relay_down, middle - 1),
        (cast == relay_up, middle),
    )
    for there, to in greeted:

        @pl.when(there)
        def _():
            pl.semaphore_signal(barrier, 1, device_id={"cast": to}, device_id_type=MESH)

    previous = {"grp": lax.rem(grp + n_grp - 1, n_grp)}
    following = {"grp": lax.rem(grp + 1, n_grp)}
    pl.semaphore_signal(barrier, 1, device_id=previous, device_id_type=MESH)

    def place(index):
        return index + tundish * (chunks - 1 - 2 * index)

    def load(chunk):
        at = pl.ds(chunk * CHUNK, CHUNK)
        return pltpu.make_async_copy(
            fields.at[0, :, at],
            first.at[:, pl.ds(2 + chunk * CHUNK, CHUNK), pl.ds(SIDE_ROWS, rows)],
            load_sem.at[chunk],
        )

    load_speed = pltpu.make_async_copy(velocity.at[0], speed, speed_sem)
    for_all = functools.partial(lax.fori_loop, 0, chunks)

    def start_load(index, carry):
        load(place(index)).start()
        return carry

    small = [
        pltpu.make_async_copy(source, target, small_sem.at[index])
        for index, (source, target) in enumerate(
            ((mask_at, mask), (diffusion_at, diffusion), (cells_at, cells), (count_at, count))
        )
    ]
    for_all(start_load, 0)
    for copy in small:
        copy.start()
    load_speed.start()

    neighbours = 1
    for there, _ in sides + bends:
        neighbours = neighbours + there.astype(jnp.int32)
    pl.semaphore_wait(barrier, neighbours)

    def pass_word(hop):
        pl.semaphore_signal(word_sem.at[hop], 1, device_id=following, device_id_type=MESH)

    pass_word(0)

    half = COMPS // 2

    def cast_copy(step, chunk, down, leg=None):
        own = (rows - 2 if down else 0) + (SIDE_ROWS if step else 0)
        start, size = (0, depth) if chunk is None else (chunk * CHUNK, CHUNK)
        at, inside = pl.ds(2 + start, size), pl.ds(start, size)
        comps = {None: pl.ds(0, COMPS), "direct": pl.ds(0, half)}.get(leg, pl.ds(half, half))
        target = (second if step else first).at[comps, at, pl.ds(SIDE_ROWS - 2 if down else below, 2)]
        if step:
            source = second.at[comps, at, pl.ds(own, 2)]
        else:
            source = fields.at[0, comps, inside, pl.ds(own, 2)]
        number = 0 if chunk is None else chunk
        sems = (cast_send.at[step, down], cast_recv.at[step, down, number])
        device = cast + 1 if down else cast - 1
        passing = relayed.at[step, :, inside]
        if leg == "there":
            target = passing
            sems = (there_send.at[step], there_recv.at[step, number])
            device = relay_down if down else relay_up
        elif leg == "on":
            source = passing
            sems = (on_send.at[step], on_recv.at[step, number])
            device = middle if down else middle - 1
        return pltpu.make_async_remote_copy(
            src_ref=source,
            dst_ref=target,
            send_sem=sems[0],
            recv_sem=sems[1],
            device_id={"cast": device},
            device_id_type=MESH,
        )

    def cast_legs(way):
        splits = above if way else below_middle
        plain = (has_down if way else has_up) & jnp.logical_not(splits)
        return ((plain, None), (splits, "direct"), (splits, "there"))

    def send_cast(step, chunk):
        for way in range(2):
            for there, leg in cast_legs(way):

                @pl.when(there)
                def _():
                    cast_copy(step, chunk, way, leg).start()

    def arrive_cast(step, chunk):
        for way in range(2):
            splits = below_middle if way else above
            plain = (has_up if way else has_down) & jnp.logical_not(splits)
            for there, leg in ((plain, None), (splits, "direct"), (splits, "on")):

                @pl.when(there)
                def _():
                    cast_copy(step, chunk, way, leg).wait_recv()

    def sent_cast(step):
        for way in range(2):
            relays = cast == (relay_down if way else relay_up)
            for there, leg in cast_legs(way) + ((relays, "on"),):

                @pl.when(there)
                def _():
                    cast_copy(step, None, way, leg).wait_send()

    def pass_on(step, chunk):
        for way in range(2):

            @pl.when(cast == (relay_down if way else relay_up))
            def _():
                cast_copy(step, chunk, way, "there").wait_recv()
                cast_copy(step, chunk, way, "on").start()

    def wid_copy(step, chunk, right):
        target = from_left if right else from_right
        at = pl.ds(0, chunks) if chunk is None else chunk
        return pltpu.make_async_remote_copy(
            src_ref=packed.at[step, at],
            dst_ref=target.at[step, at],
            send_sem=wid_send.at[step, right],
            recv_sem=wid_recv.at[step, right, 0 if chunk is None else chunk],
            device_id={"wid": wid + 1 if right else wid - 1},
            device_id_type=MESH,
        )

    def port_copy(step):
        return pltpu.make_async_remote_copy(
            src_ref=outgoing.at[step],
            dst_ref=received.at[step],
            send_sem=port_send.at[step],
            recv_sem=port_recv.at[step],
            device_id={"grp": other},
            device_id_type=MESH,
        )

    def send_wid(step, chunk):
        for way, there in enumerate((has_left, has_right)):

            @pl.when(there)
            def _():
                wid_copy(step, chunk, way).start()

    def arrive_wid(step, chunk):
        for way, there in enumerate((has_right, has_left)):

            @pl.when(there)
            def _():
                wid_copy(step, chunk, way).wait_recv()

    def sent_wid(step):
        for way, there in enumerate((has_left, has_right)):

            @pl.when(there)
            def _():
                wid_copy(step, None, way).wait_send()

    def send_first(index, carry):
        send_cast(0, place(index))
        return carry

    for_all(send_first, 0)

    lane = lax.broadcasted_iota(jnp.int32, (8, cols), 1)
    slot_lane = lane // 4

    def pack(tile_value, slot, total):
        turned = pltpu.roll(tile_value, 4 * slot + 2, 1)
        return jnp.where(slot_lane == slot, turned, total)

    def pack_first(index, carry):
        chunk = place(index)
        load(chunk).wait()
        for tile in range(tiles):
            total = jnp.zeros((8, cols), jnp.float32)
            for comp in range(COMPS):
                for at in range(CHUNK):
                    value = first[comp, 2 + chunk * CHUNK + at, pl.ds(SIDE_ROWS + tile * 8, 8)]
                    total = pack(value, comp * CHUNK + at, total)
            packed[0, chunk, tile * 8 : tile * 8 + 8] = total
        send_wid(0, chunk)
        return carry

    for_all(pack_first, 0)
    for ref in (first, second):
        for comp in range(COMPS):
            for at in (0, 1, depth + 2, depth + 3):
                ref[comp, at, SIDE_ROWS:below] = jnp.zeros((rows, cols), jnp.float32)

    for there, start in ((has_up, SIDE_ROWS - 2), (has_down, below)):

        @pl.when(jnp.logical_not(there))
        def _():
            @pl.loop(0, depth)
            def _(at):
                for ref in (first, second):
                    for comp in range(COMPS):
                        ref[comp, at + 2, start : start + 2] = jnp.zeros((2, cols), jnp.float32)

    for there, ref in ((has_left, from_left), (has_right, from_right)):

        @pl.when(jnp.logical_not(there))
        def _():
            ref[...] = jnp.zeros(ref.shape, jnp.float32)

    down, across = (lax.broadcasted_iota(jnp.int32, (2 * cols, cols), axis) for axis in (0, 1))
    apart = jnp.abs((down & (cols - 1)) - across)
    weight = jnp.where(apart == 1, 16.0, jnp.where(apart == 2, -1.0, 0.0))
    band[...] = weight.astype(jnp.bfloat16)

    for copy in small:
        copy.wait()

    for tile in range(tiles):
        liquid = jnp.zeros((8, cols), jnp.float32)
        for block in range(mask.shape[2]):
            value = 0.25 + 0.75 * mask[0, tile, block].astype(jnp.float32)
            liquid = jnp.where(lane // 16 == block, value, liquid)
        for comp in range(COMPS):
            rate[comp, tile * 8 : tile * 8 + 8] = liquid * (diffusion[0, comp] * (STEP_SIZE / 12.0))

    cell = cells[0, 0]
    cell_row, cell_col = cell >> (cols.bit_length() - 1), cell & (cols - 1)
    onehot[...] = (lax.broadcasted_iota(jnp.int32, (cols, ports), 0) == cell_col).astype(jnp.float32)
    row_hot = (lax.broadcasted_iota(jnp.int32, (rows, ports), 0) == cell_row).astype(jnp.float32)
    active = (lax.broadcasted_iota(jnp.int32, (1, ports), 1) < count[0, 0, 0]).astype(jnp.float32)
    live[0] = row_hot
    live[1] = row_hot * active
    hits[...] = lax.dot_general(
        live[1],
        onehot[...],
        (((1,), (1,)), ((), ())),
        precision=EXACT,
        preferred_element_type=jnp.float32,
    )

    def gather(step, ref):
        flat = jnp.concatenate(
            [ref[comp, 2 + surface, SIDE_ROWS:below] for comp in range(COMPS)], axis=0
        )
        wide = jnp.dot(flat, onehot[...], precision=EXACT, preferred_element_type=jnp.float32)
        for comp in range(COMPS):
            picked = wide[comp * rows : comp * rows + rows] * live[0]
            outgoing[step, comp : comp + 1] = jnp.sum(picked, axis=0, keepdims=True)

    def scatter(step):
        flat = jnp.concatenate(
            [live[1] * received[step, comp : comp + 1] for comp in range(COMPS)], axis=0
        )
        layer[...] = lax.dot_general(
            flat,
            onehot[...],
            (((1,), (1,)), ((), ())),
            precision=EXACT,
            preferred_element_type=jnp.float32,
        )

    gather(0, first)

    load_speed.wait()

    def scale(at, carry):
        speed[at] = STEP_SIZE * speed[at]
        return carry

    lax.fori_loop(0, depth, scale, 0, unroll=8)

    def rim_terms(step, chunk, own):
        place_in_slot = lane & 3
        edge = jnp.where(
            place_in_slot < 2, from_left[step, chunk, own], from_right[step, chunk, own]
        )
        after1, after2, before1, before2 = (
            pltpu.roll(edge, shift, 1) for shift in (cols - 1, cols - 2, 1, 2)
        )
        near = jnp.where(place_in_slot == 1, after1, jnp.where(place_in_slot == 2, before1, 0.0))
        return 16.0 * near - jnp.where(place_in_slot < 2, after2, before2)

    at_rim = (lane < 2) | (lane >= cols - 2)

    def advance(step, chunk):
        source = second if step else first
        base = chunk * CHUNK
        owns = [pl.ds(tile * 8, 8) for tile in range(tiles)]
        rims = [rim_terms(step, chunk, own) for own in owns]
        totals = [jnp.zeros((8, cols), jnp.float32) for _ in owns]
        for comp in range(COMPS):
            block = source[comp, pl.ds(base + 2, CHUNK), pl.ds(SIDE_ROWS, rows)]
            block = block.reshape(CHUNK * rows, cols)
            high = block.astype(jnp.bfloat16)
            low = (block - high.astype(jnp.float32)).astype(jnp.bfloat16)
            width = jnp.dot(
                jnp.concatenate([high, low], axis=1),
                band[...],
                preferred_element_type=jnp.float32,
            )
            for tile, own in enumerate(owns):
                at_row = SIDE_ROWS + tile * 8
                factor = rate[comp, own]
                column = [
                    source[comp, base + at, pl.ds(at_row, 8)] for at in range(CHUNK + 4)
                ]
                for at in range(CHUNK):
                    slot = comp * CHUNK + at
                    here = base + 2 + at
                    value = column[at + 2]
                    up1, up2, down1, down2 = (
                        source[comp, here, pl.ds(at_row + shift, 8)] for shift in (-1, -2, 1, 2)
                    )
                    side = pltpu.roll(rims[tile], (cols - 4 * slot - 2) % cols, 1)
                    start = at * rows + tile * 8
                    sideways = width[start : start + 8] + jnp.where(at_rim, side, 0.0)
                    near = (up1 + down1) + (column[at + 1] + column[at + 3])
                    far = (up2 + down2) + (column[at] + column[at + 4])
                    laplace = (16.0 * near - far) + (sideways - 90.0 * value)
                    flow = speed[base + at, own] * (value - up1)
                    fresh = value + (factor * laplace - flow)
                    if step:
                        result[comp, base + at, own] = fresh
                    else:
                        second[comp, here, pl.ds(at_row, 8)] = fresh
                        totals[tile] = pack(fresh, slot, totals[tile])
        if not step:
            for own, total in zip(owns, totals):
                packed[1, chunk, own] = total

    def step_one(index, carry):
        chunk = place(index)
        pass_on(0, chunk)
        arrive_wid(0, chunk)
        arrive_cast(0, chunk)
        advance(0, chunk)
        send_cast(1, chunk)
        send_wid(1, chunk)
        for hop in range(n_grp // 2):

            @pl.when(index == 2 * hop + 1)
            def _():
                pl.semaphore_wait(word_sem.at[hop], 1)
                if hop + 1 < n_grp // 2:
                    pass_word(hop + 1)
                else:
                    port_copy(0).start()

        return carry

    for_all(step_one, 0)

    port_copy(0).wait_recv()
    scatter(0)
    inner = pl.ds(SIDE_ROWS + 2, rows - 4)
    for comp in range(COMPS):
        old = second[comp, 2 + surface, inner]
        change = layer[comp * rows + 2 : comp * rows + rows - 2] - hits[2 : rows - 2] * old
        second[comp, 2 + surface, inner] = old + RELAXATION * change
    gather(1, second)
    port_copy(1).start()

    def step_two(index, carry):
        chunk = place(index)
        pass_on(1, chunk)
        arrive_wid(1, chunk)
        arrive_cast(1, chunk)
        advance(1, chunk)
        return carry

    for_all(step_two, 0)

    port_copy(1).wait_recv()
    scatter(1)
    for comp in range(COMPS):
        old = result[comp, surface]
        change = layer[comp * rows : comp * rows + rows] - hits[...] * old
        result[comp, surface] = old + RELAXATION * change

    for step in range(2):
        sent_cast(step)
        sent_wid(step)
    for step in range(2):
        port_copy(step).wait_send()


def per_device(fields, velocity, liquid_mask, diffusion, port_cell, handoff_count):
    _, comps, depth, rows, cols = fields.shape
    ports = port_cell.shape[-1]
    chunks = depth // CHUNK
    f32 = jnp.float32
    padded = pltpu.VMEM((comps, depth + 4, rows + 2 * SIDE_ROWS, cols), f32)
    strips = pltpu.VMEM((2, chunks, rows, cols), f32)
    dma = pltpu.SemaphoreType.DMA
    return pl.pallas_call(
        kernel,
        out_shape=pltpu.VMEM(fields.shape, f32),
        in_specs=[pl.BlockSpec(memory_space=pltpu.HBM)] * 6,
        out_specs=pl.BlockSpec(memory_space=pltpu.VMEM),
        scratch_shapes=[
            padded,
            padded,
            pltpu.VMEM((depth, rows, cols), f32),
            pltpu.SMEM(liquid_mask.shape, jnp.int32),
            pltpu.SMEM(diffusion.shape, f32),
            pltpu.VMEM(port_cell.shape, jnp.int32),
            pltpu.SMEM(handoff_count.shape, jnp.int32),
            pltpu.VMEM((comps, rows, cols), f32),
            pltpu.VMEM((2 * cols, cols), jnp.bfloat16),
            strips,
            strips,
            strips,
            pltpu.VMEM((cols, ports), f32),
            pltpu.VMEM((2, rows, ports), f32),
            pltpu.VMEM((comps * rows, cols), f32),
            pltpu.VMEM((rows, cols), f32),
            pltpu.VMEM((2, comps, ports), f32),
            pltpu.VMEM((2, comps, ports), f32),
            pltpu.VMEM((2, comps // 2, depth, 2, cols), f32),
            dma((chunks,)),
            dma,
            dma((4,)),
            dma((2, 2)),
            dma((2, 2, chunks)),
            dma((2, 2)),
            dma((2, 2, chunks)),
            dma((2,)),
            dma((2,)),
            pltpu.SemaphoreType.REGULAR((lax.axis_size("grp") // 2,)),
            dma((2,)),
            dma((2, chunks)),
            dma((2,)),
            dma((2, chunks)),
        ],
        compiler_params=pltpu.CompilerParams(
            collective_id=0, has_side_effects=True, vmem_limit_bytes=54 * 2**20
        ),
        cost_estimate=pl.CostEstimate(
            flops=60 * fields.size, bytes_accessed=9 * 2**20, transcendentals=0
        ),
    )(fields, velocity, liquid_mask, diffusion, port_cell, handoff_count)


def solution(mesh):
    in_specs = (
        P("grp", None, None, "cast", "wid"),
        P("grp", None, "cast", "wid"),
        P("grp", "cast", "wid"),
        P("grp", None),
        P("grp", "cast", "wid", None),
        P("grp", "cast", "wid"),
    )
    out_specs = P("grp", None, None, "cast", "wid")
    return jax.shard_map(
        per_device, mesh=mesh, in_specs=in_specs, out_specs=out_specs, check_vma=False
    )
```

```python
import functools

import jax
import jax.numpy as jnp
from jax import lax
from jax.experimental import pallas as pl
from jax.experimental.pallas import tpu as pltpu
from jax.sharding import PartitionSpec as P

STEP_SIZE = 0.1
RELAXATION = 0.5
COMPS = 4
CHUNK = 8
SIDE_ROWS = 8
AHEAD = 2
BEHIND = 4
MESH = pl.DeviceIdType.MESH
EXACT = lax.Precision.HIGHEST


def kernel(
    fields,
    velocity,
    mask_at,
    diffusion_at,
    cells_at,
    count_at,
    out,
    first,
    second,
    speed,
    mask,
    diffusion,
    cells,
    count,
    rate,
    band,
    packed,
    from_left,
    from_right,
    onehot,
    live,
    layer,
    hits,
    outgoing,
    received,
    relayed,
    load_sem,
    speed_sem,
    small_sem,
    cast_send,
    cast_recv,
    wid_send,
    wid_recv,
    port_send,
    port_recv,
    word_sem,
    there_send,
    there_recv,
    on_send,
    on_recv,
):
    depth, rows, cols = fields.shape[2:]
    ports = cells.shape[-1]
    chunks = depth // CHUNK
    result = out.at[0]
    tiles = rows // 8
    below = SIDE_ROWS + rows
    grp, cast, wid = (lax.axis_index(name) for name in ("grp", "cast", "wid"))
    n_grp, n_cast, n_wid = (lax.axis_size(name) for name in ("grp", "cast", "wid"))
    other = lax.rem(grp + n_grp // 2, n_grp)
    tundish = (grp < n_grp // 2).astype(jnp.int32)
    surface = tundish * (depth - 1)
    has_up, has_down = cast > 0, cast < n_cast - 1
    has_left, has_right = wid > 0, wid < n_wid - 1
    sides = (
        (has_up, {"cast": cast - 1}),
        (has_down, {"cast": cast + 1}),
        (has_left, {"wid": wid - 1}),
        (has_right, {"wid": wid + 1}),
    )

    barrier = pltpu.get_barrier_semaphore()
    for there, device in sides:

        @pl.when(there)
        def _():
            pl.semaphore_signal(barrier, 1, device_id=device, device_id_type=MESH)

    middle = n_cast // 2
    above, below_middle = cast == middle - 1, cast == middle
    relay_down, relay_up = (n_cast - 1, 0)
    bends = (
        (above, relay_down),
        (below_middle, relay_up),
        (cast == relay_down, middle),
        (cast == relay_up, middle - 1),
    )
    greeted = (
        (above, relay_up),
        (below_middle, relay_down),
        (cast == relay_down, middle - 1),
        (cast == relay_up, middle),
    )
    for there, to in greeted:

        @pl.when(there)
        def _():
            pl.semaphore_signal(barrier, 1, device_id={"cast": to}, device_id_type=MESH)

    bay = grp < n_grp // 2
    strand = jnp.logical_not(bay)

    @pl.when(bay)
    def _():
        pl.semaphore_signal(barrier, 1, device_id={"grp": other}, device_id_type=MESH)

    def place(index):
        return index + tundish * (chunks - 1 - 2 * index)

    def load(chunk):
        at = pl.ds(chunk * CHUNK, CHUNK)
        return pltpu.make_async_copy(
            fields.at[0, :, at],
            first.at[:, pl.ds(2 + chunk * CHUNK, CHUNK), pl.ds(SIDE_ROWS, rows)],
            load_sem.at[chunk],
        )

    load_speed = pltpu.make_async_copy(velocity.at[0], speed, speed_sem)
    for_all = functools.partial(lax.fori_loop, 0, chunks)

    def start_load(index, carry):
        load(place(index)).start()
        return carry

    small = [
        pltpu.make_async_copy(source, target, small_sem.at[index])
        for index, (source, target) in enumerate(
            ((mask_at, mask), (diffusion_at, diffusion), (cells_at, cells), (count_at, count))
        )
    ]
    for_all(start_load, 0)
    for copy in small:
        copy.start()
    load_speed.start()

    neighbours = strand.astype(jnp.int32)
    for there, _ in sides + bends:
        neighbours = neighbours + there.astype(jnp.int32)
    pl.semaphore_wait(barrier, neighbours)

    @pl.when(strand)
    def _():
        pl.semaphore_signal(word_sem, 1, device_id={"grp": other}, device_id_type=MESH)

    half = COMPS // 2

    def cast_copy(step, chunk, down, leg=None):
        own = (rows - 2 if down else 0) + (SIDE_ROWS if step else 0)
        start, size = (0, depth) if chunk is None else (chunk * CHUNK, CHUNK)
        at, inside = pl.ds(2 + start, size), pl.ds(start, size)
        comps = {None: pl.ds(0, COMPS), "direct": pl.ds(0, half)}.get(leg, pl.ds(half, half))
        target = (second if step else first).at[comps, at, pl.ds(SIDE_ROWS - 2 if down else below, 2)]
        if step:
            source = second.at[comps, at, pl.ds(own, 2)]
        else:
            source = fields.at[0, comps, inside, pl.ds(own, 2)]
        number = 0 if chunk is None else chunk
        sems = (cast_send.at[step, down], cast_recv.at[step, down, number])
        device = cast + 1 if down else cast - 1
        passing = relayed.at[step, :, inside]
        if leg == "there":
            target = passing
            sems = (there_send.at[step], there_recv.at[step, number])
            device = relay_down if down else relay_up
        elif leg == "on":
            source = passing
            sems = (on_send.at[step], on_recv.at[step, number])
            device = middle if down else middle - 1
        return pltpu.make_async_remote_copy(
            src_ref=source,
            dst_ref=target,
            send_sem=sems[0],
            recv_sem=sems[1],
            device_id={"cast": device},
            device_id_type=MESH,
        )

    def cast_legs(way):
        splits = above if way else below_middle
        plain = (has_down if way else has_up) & jnp.logical_not(splits)
        return ((plain, None), (splits, "there"), (splits, "direct"))

    def send_cast(step, chunk, which=slice(None)):
        for way in range(2):
            for there, leg in cast_legs(way)[which]:

                @pl.when(there)
                def _():
                    cast_copy(step, chunk, way, leg).start()

    def arrive_cast(step, chunk):
        for way in range(2):
            splits = below_middle if way else above
            plain = (has_up if way else has_down) & jnp.logical_not(splits)
            for there, leg in ((plain, None), (splits, "direct"), (splits, "on")):

                @pl.when(there)
                def _():
                    cast_copy(step, chunk, way, leg).wait_recv()

    def sent_cast(step):
        for way in range(2):
            relays = cast == (relay_down if way else relay_up)
            for there, leg in cast_legs(way) + ((relays, "on"),):

                @pl.when(there)
                def _():
                    cast_copy(step, None, way, leg).wait_send()

    def pass_on(step, chunk):
        for way in range(2):

            @pl.when(cast == (relay_down if way else relay_up))
            def _():
                cast_copy(step, chunk, way, "there").wait_recv()
                cast_copy(step, chunk, way, "on").start()

    def wid_copy(step, chunk, right):
        target = from_left if right else from_right
        at = pl.ds(0, chunks) if chunk is None else chunk
        return pltpu.make_async_remote_copy(
            src_ref=packed.at[step, at],
            dst_ref=target.at[step, at],
            send_sem=wid_send.at[step, right],
            recv_sem=wid_recv.at[step, right, 0 if chunk is None else chunk],
            device_id={"wid": wid + 1 if right else wid - 1},
            device_id_type=MESH,
        )

    def port_copy(step):
        return pltpu.make_async_remote_copy(
            src_ref=outgoing.at[step],
            dst_ref=received.at[step],
            send_sem=port_send.at[step],
            recv_sem=port_recv.at[step],
            device_id={"grp": other},
            device_id_type=MESH,
        )

    def send_wid(step, chunk):
        for way, there in enumerate((has_left, has_right)):

            @pl.when(there)
            def _():
                wid_copy(step, chunk, way).start()

    def arrive_wid(step, chunk):
        for way, there in enumerate((has_right, has_left)):

            @pl.when(there)
            def _():
                wid_copy(step, chunk, way).wait_recv()

    def sent_wid(step):
        for way, there in enumerate((has_left, has_right)):

            @pl.when(there)
            def _():
                wid_copy(step, None, way).wait_send()

    def send_first(index, carry):
        send_cast(0, place(index), slice(0, 2))
        return carry

    for_all(send_first, 0)

    lane = lax.broadcasted_iota(jnp.int32, (8, cols), 1)
    slot_lane = lane // 4

    def pack(tile_value, slot, total):
        turned = pltpu.roll(tile_value, 4 * slot + 2, 1)
        return jnp.where(slot_lane == slot, turned, total)

    def pack_first(index, carry):
        chunk = place(index)
        load(chunk).wait()
        for tile in range(tiles):
            total = jnp.zeros((8, cols), jnp.float32)
            for comp in range(COMPS):
                for at in range(CHUNK):
                    value = first[comp, 2 + chunk * CHUNK + at, pl.ds(SIDE_ROWS + tile * 8, 8)]
                    total = pack(value, comp * CHUNK + at, total)
            packed[0, chunk, tile * 8 : tile * 8 + 8] = total
        send_wid(0, chunk)
        return carry

    for_all(pack_first, 0)

    def send_legs(index, carry):
        send_cast(0, place(index), slice(2, 3))
        return carry

    for_all(send_legs, 0)
    for ref in (first, second):
        for comp in range(COMPS):
            for at in (0, 1, depth + 2, depth + 3):
                ref[comp, at, SIDE_ROWS:below] = jnp.zeros((rows, cols), jnp.float32)

    for there, start in ((has_up, SIDE_ROWS - 2), (has_down, below)):

        @pl.when(jnp.logical_not(there))
        def _():
            @pl.loop(0, depth)
            def _(at):
                for ref in (first, second):
                    for comp in range(COMPS):
                        ref[comp, at + 2, start : start + 2] = jnp.zeros((2, cols), jnp.float32)

    for there, ref in ((has_left, from_left), (has_right, from_right)):

        @pl.when(jnp.logical_not(there))
        def _():
            ref[...] = jnp.zeros(ref.shape, jnp.float32)

    down, across = (lax.broadcasted_iota(jnp.int32, (2 * cols, cols), axis) for axis in (0, 1))
    apart = jnp.abs((down & (cols - 1)) - across)
    weight = jnp.where(apart == 1, 16.0, jnp.where(apart == 2, -1.0, 0.0))
    band[...] = weight.astype(jnp.bfloat16)

    for copy in small:
        copy.wait()

    for tile in range(tiles):
        liquid = jnp.zeros((8, cols), jnp.float32)
        for block in range(mask.shape[2]):
            value = 0.25 + 0.75 * mask[0, tile, block].astype(jnp.float32)
            liquid = jnp.where(lane // 16 == block, value, liquid)
        for comp in range(COMPS):
            rate[comp, tile * 8 : tile * 8 + 8] = liquid * (diffusion[0, comp] * (STEP_SIZE / 12.0))

    cell = cells[0, 0]
    cell_row, cell_col = cell >> (cols.bit_length() - 1), cell & (cols - 1)
    onehot[...] = (lax.broadcasted_iota(jnp.int32, (cols, ports), 0) == cell_col).astype(jnp.float32)
    row_hot = (lax.broadcasted_iota(jnp.int32, (rows, ports), 0) == cell_row).astype(jnp.float32)
    active = (lax.broadcasted_iota(jnp.int32, (1, ports), 1) < count[0, 0, 0]).astype(jnp.float32)
    live[0] = row_hot
    live[1] = row_hot * active
    hits[...] = lax.dot_general(
        live[1],
        onehot[...],
        (((1,), (1,)), ((), ())),
        precision=EXACT,
        preferred_element_type=jnp.float32,
    )

    def gather(step, ref):
        flat = jnp.concatenate(
            [ref[comp, 2 + surface, SIDE_ROWS:below] for comp in range(COMPS)], axis=0
        )
        wide = jnp.dot(flat, onehot[...], precision=EXACT, preferred_element_type=jnp.float32)
        for comp in range(COMPS):
            picked = wide[comp * rows : comp * rows + rows] * live[0]
            outgoing[step, comp : comp + 1] = jnp.sum(picked, axis=0, keepdims=True)

    def scatter(step):
        flat = jnp.concatenate(
            [live[1] * received[step, comp : comp + 1] for comp in range(COMPS)], axis=0
        )
        layer[...] = lax.dot_general(
            flat,
            onehot[...],
            (((1,), (1,)), ((), ())),
            precision=EXACT,
            preferred_element_type=jnp.float32,
        )

    gather(0, first)

    load_speed.wait()

    def scale(at, carry):
        speed[at] = STEP_SIZE * speed[at]
        return carry

    lax.fori_loop(0, depth, scale, 0, unroll=8)

    def rim_terms(step, chunk, own):
        place_in_slot = lane & 3
        edge = jnp.where(
            place_in_slot < 2, from_left[step, chunk, own], from_right[step, chunk, own]
        )
        after1, after2, before1, before2 = (
            pltpu.roll(edge, shift, 1) for shift in (cols - 1, cols - 2, 1, 2)
        )
        near = jnp.where(place_in_slot == 1, after1, jnp.where(place_in_slot == 2, before1, 0.0))
        return 16.0 * near - jnp.where(place_in_slot < 2, after2, before2)

    at_rim = (lane < 2) | (lane >= cols - 2)

    def advance(step, chunk):
        source = second if step else first
        base = chunk * CHUNK
        owns = [pl.ds(tile * 8, 8) for tile in range(tiles)]
        rims = [rim_terms(step, chunk, own) for own in owns]
        totals = [jnp.zeros((8, cols), jnp.float32) for _ in owns]
        for comp in range(COMPS):
            block = source[comp, pl.ds(base + 2, CHUNK), pl.ds(SIDE_ROWS, rows)]
            block = block.reshape(CHUNK * rows, cols)
            high = block.astype(jnp.bfloat16)
            low = (block - high.astype(jnp.float32)).astype(jnp.bfloat16)
            width = jnp.dot(
                jnp.concatenate([high, low], axis=1),
                band[...],
                preferred_element_type=jnp.float32,
            )
            for tile, own in enumerate(owns):
                at_row = SIDE_ROWS + tile * 8
                factor = rate[comp, own]
                column = [
                    source[comp, base + at, pl.ds(at_row, 8)] for at in range(CHUNK + 4)
                ]
                for at in range(CHUNK):
                    slot = comp * CHUNK + at
                    here = base + 2 + at
                    value = column[at + 2]
                    up1, up2, down1, down2 = (
                        source[comp, here, pl.ds(at_row + shift, 8)] for shift in (-1, -2, 1, 2)
                    )
                    side = pltpu.roll(rims[tile], (cols - 4 * slot - 2) % cols, 1)
                    start = at * rows + tile * 8
                    sideways = width[start : start + 8] + jnp.where(at_rim, side, 0.0)
                    near = (up1 + down1) + (column[at + 1] + column[at + 3])
                    far = (up2 + down2) + (column[at] + column[at + 4])
                    laplace = (16.0 * near - far) + (sideways - 90.0 * value)
                    flow = speed[base + at, own] * (value - up1)
                    fresh = value + (factor * laplace - flow)
                    if step:
                        result[comp, base + at, own] = fresh
                    else:
                        second[comp, here, pl.ds(at_row, 8)] = fresh
                        totals[tile] = pack(fresh, slot, totals[tile])
        if not step:
            for own, total in zip(owns, totals):
                packed[1, chunk, own] = total

    for index in range(AHEAD):
        pass_on(0, place(index))

    def step_one(index, carry):
        chunk = place(index)

        @pl.when(index + AHEAD < chunks)
        def _():
            pass_on(0, place(index + AHEAD))

        arrive_wid(0, chunk)
        arrive_cast(0, chunk)
        advance(0, chunk)
        send_cast(1, chunk)
        send_wid(1, chunk)
        @pl.when((index == chunks // 2) & bay)
        def _():
            pl.semaphore_wait(word_sem, 1)

        @pl.when(index == chunks // 2)
        def _():
            port_copy(0).start()

        return carry

    for_all(step_one, 0)

    port_copy(0).wait_recv()
    scatter(0)
    inner = pl.ds(SIDE_ROWS + 2, rows - 4)
    for comp in range(COMPS):
        old = second[comp, 2 + surface, inner]
        change = layer[comp * rows + 2 : comp * rows + rows - 2] - hits[2 : rows - 2] * old
        second[comp, 2 + surface, inner] = old + RELAXATION * change
    gather(1, second)
    port_copy(1).start()

    def step_two(index, carry):
        chunk = place(index)
        pass_on(1, chunk)
        arrive_wid(1, chunk)
        arrive_cast(1, chunk)
        advance(1, chunk)

        @pl.when(index == chunks - 4)
        def _():
            port_copy(1).wait_recv()
            scatter(1)
            for comp in range(COMPS):
                old = result[comp, surface]
                change = layer[comp * rows : comp * rows + rows] - hits[...] * old
                result[comp, surface] = old + RELAXATION * change

        return carry

    for_all(step_two, 0)

    for step in range(2):
        sent_cast(step)
        sent_wid(step)
    for step in range(2):
        port_copy(step).wait_send()


def per_device(fields, velocity, liquid_mask, diffusion, port_cell, handoff_count):
    _, comps, depth, rows, cols = fields.shape
    ports = port_cell.shape[-1]
    chunks = depth // CHUNK
    f32 = jnp.float32
    padded = pltpu.VMEM((comps, depth + 4, rows + 2 * SIDE_ROWS, cols), f32)
    strips = pltpu.VMEM((2, chunks, rows, cols), f32)
    dma = pltpu.SemaphoreType.DMA
    return pl.pallas_call(
        kernel,
        out_shape=pltpu.VMEM(fields.shape, f32),
        in_specs=[pl.BlockSpec(memory_space=pltpu.HBM)] * 6,
        out_specs=pl.BlockSpec(memory_space=pltpu.VMEM),
        scratch_shapes=[
            padded,
            padded,
            pltpu.VMEM((depth, rows, cols), f32),
            pltpu.SMEM(liquid_mask.shape, jnp.int32),
            pltpu.SMEM(diffusion.shape, f32),
            pltpu.VMEM(port_cell.shape, jnp.int32),
            pltpu.SMEM(handoff_count.shape, jnp.int32),
            pltpu.VMEM((comps, rows, cols), f32),
            pltpu.VMEM((2 * cols, cols), jnp.bfloat16),
            strips,
            strips,
            strips,
            pltpu.VMEM((cols, ports), f32),
            pltpu.VMEM((2, rows, ports), f32),
            pltpu.VMEM((comps * rows, cols), f32),
            pltpu.VMEM((rows, cols), f32),
            pltpu.VMEM((2, comps, ports), f32),
            pltpu.VMEM((2, comps, ports), f32),
            pltpu.VMEM((2, comps // 2, depth, 2, cols), f32),
            dma((chunks,)),
            dma,
            dma((4,)),
            dma((2, 2)),
            dma((2, 2, chunks)),
            dma((2, 2)),
            dma((2, 2, chunks)),
            dma((2,)),
            dma((2,)),
            pltpu.SemaphoreType.REGULAR,
            dma((2,)),
            dma((2, chunks)),
            dma((2,)),
            dma((2, chunks)),
        ],
        compiler_params=pltpu.CompilerParams(
            collective_id=0, has_side_effects=True, vmem_limit_bytes=54 * 2**20
        ),
        cost_estimate=pl.CostEstimate(
            flops=60 * fields.size, bytes_accessed=9 * 2**20, transcendentals=0
        ),
    )(fields, velocity, liquid_mask, diffusion, port_cell, handoff_count)


def solution(mesh):
    in_specs = (
        P("grp", None, None, "cast", "wid"),
        P("grp", None, "cast", "wid"),
        P("grp", "cast", "wid"),
        P("grp", None),
        P("grp", "cast", "wid", None),
        P("grp", "cast", "wid"),
    )
    out_specs = P("grp", None, None, "cast", "wid")
    return jax.shard_map(
        per_device, mesh=mesh, in_specs=in_specs, out_specs=out_specs, check_vma=False
    )
```

```python
import functools

import jax
import jax.numpy as jnp
from jax import lax
from jax.experimental import pallas as pl
from jax.experimental.pallas import tpu as pltpu
from jax.sharding import PartitionSpec as P

STEP_SIZE = 0.1
RELAXATION = 0.5
COMPS = 4
CHUNK = 8
SIDE_ROWS = 8
AHEAD = 4
AHEAD_AGAIN = 8
MESH = pl.DeviceIdType.MESH
EXACT = lax.Precision.HIGHEST


def kernel(
    fields,
    velocity,
    mask_at,
    diffusion_at,
    cells_at,
    count_at,
    out,
    first,
    second,
    speed,
    mask,
    diffusion,
    cells,
    count,
    rate,
    band,
    packed,
    from_left,
    from_right,
    onehot,
    live,
    layer,
    hits,
    outgoing,
    received,
    relayed,
    load_sem,
    speed_sem,
    small_sem,
    cast_send,
    cast_recv,
    wid_send,
    wid_recv,
    port_send,
    port_recv,
    word_sem,
    there_send,
    there_recv,
    on_send,
    on_recv,
):
    depth, rows, cols = fields.shape[2:]
    ports = cells.shape[-1]
    chunks = depth // CHUNK
    result = out.at[0]
    tiles = rows // 8
    below = SIDE_ROWS + rows
    grp, cast, wid = (lax.axis_index(name) for name in ("grp", "cast", "wid"))
    n_grp, n_cast, n_wid = (lax.axis_size(name) for name in ("grp", "cast", "wid"))
    other = lax.rem(grp + n_grp // 2, n_grp)
    tundish = (grp < n_grp // 2).astype(jnp.int32)
    surface = tundish * (depth - 1)
    has_up, has_down = cast > 0, cast < n_cast - 1
    has_left, has_right = wid > 0, wid < n_wid - 1
    sides = (
        (has_up, {"cast": cast - 1}),
        (has_down, {"cast": cast + 1}),
        (has_left, {"wid": wid - 1}),
        (has_right, {"wid": wid + 1}),
    )

    barrier = pltpu.get_barrier_semaphore()
    for there, device in sides:

        @pl.when(there)
        def _():
            pl.semaphore_signal(barrier, 1, device_id=device, device_id_type=MESH)

    middle = n_cast // 2
    above, below_middle = cast == middle - 1, cast == middle
    relay_down, relay_up = (n_cast - 1, 0)
    bends = (
        (above, relay_down),
        (below_middle, relay_up),
        (cast == relay_down, middle),
        (cast == relay_up, middle - 1),
    )
    greeted = (
        (above, relay_up),
        (below_middle, relay_down),
        (cast == relay_down, middle - 1),
        (cast == relay_up, middle),
    )
    for there, to in greeted:

        @pl.when(there)
        def _():
            pl.semaphore_signal(barrier, 1, device_id={"cast": to}, device_id_type=MESH)

    bay = grp < n_grp // 2
    strand = jnp.logical_not(bay)

    @pl.when(bay)
    def _():
        pl.semaphore_signal(barrier, 1, device_id={"grp": other}, device_id_type=MESH)

    def place(index):
        return index + tundish * (chunks - 1 - 2 * index)

    def load(chunk):
        at = pl.ds(chunk * CHUNK, CHUNK)
        return pltpu.make_async_copy(
            fields.at[0, :, at],
            first.at[:, pl.ds(2 + chunk * CHUNK, CHUNK), pl.ds(SIDE_ROWS, rows)],
            load_sem.at[chunk],
        )

    load_speed = pltpu.make_async_copy(velocity.at[0], speed, speed_sem)
    for_all = functools.partial(lax.fori_loop, 0, chunks)

    def start_load(index, carry):
        load(place(index)).start()
        return carry

    small = [
        pltpu.make_async_copy(source, target, small_sem.at[index])
        for index, (source, target) in enumerate(
            ((mask_at, mask), (diffusion_at, diffusion), (cells_at, cells), (count_at, count))
        )
    ]
    for_all(start_load, 0)
    for copy in small:
        copy.start()
    load_speed.start()

    neighbours = strand.astype(jnp.int32)
    for there, _ in sides + bends:
        neighbours = neighbours + there.astype(jnp.int32)
    pl.semaphore_wait(barrier, neighbours)

    @pl.when(strand)
    def _():
        pl.semaphore_signal(word_sem, 1, device_id={"grp": other}, device_id_type=MESH)

    half = COMPS // 2

    def cast_copy(step, chunk, down, leg=None):
        own = (rows - 2 if down else 0) + (SIDE_ROWS if step else 0)
        start, size = (0, depth) if chunk is None else (chunk * CHUNK, CHUNK)
        at, inside = pl.ds(2 + start, size), pl.ds(start, size)
        comps = {None: pl.ds(0, COMPS), "direct": pl.ds(0, half)}.get(leg, pl.ds(half, half))
        target = (second if step else first).at[comps, at, pl.ds(SIDE_ROWS - 2 if down else below, 2)]
        if step:
            source = second.at[comps, at, pl.ds(own, 2)]
        else:
            source = fields.at[0, comps, inside, pl.ds(own, 2)]
        number = 0 if chunk is None else chunk
        sems = (cast_send.at[step, down], cast_recv.at[step, down, number])
        device = cast + 1 if down else cast - 1
        passing = relayed.at[step, :, inside]
        if leg == "there":
            target = passing
            sems = (there_send.at[step], there_recv.at[step, number])
            device = relay_down if down else relay_up
        elif leg == "on":
            source = passing
            sems = (on_send.at[step], on_recv.at[step, number])
            device = middle if down else middle - 1
        return pltpu.make_async_remote_copy(
            src_ref=source,
            dst_ref=target,
            send_sem=sems[0],
            recv_sem=sems[1],
            device_id={"cast": device},
            device_id_type=MESH,
        )

    def cast_legs(way):
        splits = above if way else below_middle
        plain = (has_down if way else has_up) & jnp.logical_not(splits)
        return ((plain, None), (splits, "there"), (splits, "direct"))

    def send_cast(step, chunk, which=slice(None)):
        for way in range(2):
            for there, leg in cast_legs(way)[which]:

                @pl.when(there)
                def _():
                    cast_copy(step, chunk, way, leg).start()

    def arrive_cast(step, chunk):
        for way in range(2):
            splits = below_middle if way else above
            plain = (has_up if way else has_down) & jnp.logical_not(splits)
            for there, leg in ((plain, None), (splits, "direct"), (splits, "on")):

                @pl.when(there)
                def _():
                    cast_copy(step, chunk, way, leg).wait_recv()

    def sent_cast(step):
        for way in range(2):
            relays = cast == (relay_down if way else relay_up)
            for there, leg in cast_legs(way) + ((relays, "on"),):

                @pl.when(there)
                def _():
                    cast_copy(step, None, way, leg).wait_send()

    def pass_on(step, chunk):
        for way in range(2):

            @pl.when(cast == (relay_down if way else relay_up))
            def _():
                cast_copy(step, chunk, way, "there").wait_recv()
                cast_copy(step, chunk, way, "on").start()

    def wid_copy(step, chunk, right):
        target = from_left if right else from_right
        at = pl.ds(0, chunks) if chunk is None else chunk
        return pltpu.make_async_remote_copy(
            src_ref=packed.at[step, at],
            dst_ref=target.at[step, at],
            send_sem=wid_send.at[step, right],
            recv_sem=wid_recv.at[step, right, 0 if chunk is None else chunk],
            device_id={"wid": wid + 1 if right else wid - 1},
            device_id_type=MESH,
        )

    def port_copy(step):
        return pltpu.make_async_remote_copy(
            src_ref=outgoing.at[step],
            dst_ref=received.at[step],
            send_sem=port_send.at[step],
            recv_sem=port_recv.at[step],
            device_id={"grp": other},
            device_id_type=MESH,
        )

    def send_wid(step, chunk):
        for way, there in enumerate((has_left, has_right)):

            @pl.when(there)
            def _():
                wid_copy(step, chunk, way).start()

    def arrive_wid(step, chunk):
        for way, there in enumerate((has_right, has_left)):

            @pl.when(there)
            def _():
                wid_copy(step, chunk, way).wait_recv()

    def sent_wid(step):
        for way, there in enumerate((has_left, has_right)):

            @pl.when(there)
            def _():
                wid_copy(step, None, way).wait_send()

    def send_first(index, carry):
        send_cast(0, place(index), slice(0, 2))
        return carry

    for_all(send_first, 0)

    lane = lax.broadcasted_iota(jnp.int32, (8, cols), 1)
    slot_lane = lane // 4

    def pack(tile_value, slot, total):
        turned = pltpu.roll(tile_value, 4 * slot + 2, 1)
        return jnp.where(slot_lane == slot, turned, total)

    def pack_first(index, carry):
        chunk = place(index)
        load(chunk).wait()
        for tile in range(tiles):
            total = jnp.zeros((8, cols), jnp.float32)
            for comp in range(COMPS):
                for at in range(CHUNK):
                    value = first[comp, 2 + chunk * CHUNK + at, pl.ds(SIDE_ROWS + tile * 8, 8)]
                    total = pack(value, comp * CHUNK + at, total)
            packed[0, chunk, tile * 8 : tile * 8 + 8] = total
        send_wid(0, chunk)
        return carry

    for_all(pack_first, 0)

    def send_legs(index, carry):
        send_cast(0, place(index), slice(2, 3))
        return carry

    for_all(send_legs, 0)
    for ref in (first, second):
        for comp in range(COMPS):
            for at in (0, 1, depth + 2, depth + 3):
                ref[comp, at, SIDE_ROWS:below] = jnp.zeros((rows, cols), jnp.float32)

    for there, start in ((has_up, SIDE_ROWS - 2), (has_down, below)):

        @pl.when(jnp.logical_not(there))
        def _():
            @pl.loop(0, depth)
            def _(at):
                for ref in (first, second):
                    for comp in range(COMPS):
                        ref[comp, at + 2, start : start + 2] = jnp.zeros((2, cols), jnp.float32)

    for there, ref in ((has_left, from_left), (has_right, from_right)):

        @pl.when(jnp.logical_not(there))
        def _():
            ref[...] = jnp.zeros(ref.shape, jnp.float32)

    down, across = (lax.broadcasted_iota(jnp.int32, (2 * cols, cols), axis) for axis in (0, 1))
    apart = jnp.abs((down & (cols - 1)) - across)
    weight = jnp.where(apart == 1, 16.0, jnp.where(apart == 2, -1.0, 0.0))
    band[...] = weight.astype(jnp.bfloat16)

    for copy in small:
        copy.wait()

    for tile in range(tiles):
        liquid = jnp.zeros((8, cols), jnp.float32)
        for block in range(mask.shape[2]):
            value = 0.25 + 0.75 * mask[0, tile, block].astype(jnp.float32)
            liquid = jnp.where(lane // 16 == block, value, liquid)
        for comp in range(COMPS):
            rate[comp, tile * 8 : tile * 8 + 8] = liquid * (diffusion[0, comp] * (STEP_SIZE / 12.0))

    cell = cells[0, 0]
    cell_row, cell_col = cell >> (cols.bit_length() - 1), cell & (cols - 1)
    onehot[...] = (lax.broadcasted_iota(jnp.int32, (cols, ports), 0) == cell_col).astype(jnp.float32)
    row_hot = (lax.broadcasted_iota(jnp.int32, (rows, ports), 0) == cell_row).astype(jnp.float32)
    active = (lax.broadcasted_iota(jnp.int32, (1, ports), 1) < count[0, 0, 0]).astype(jnp.float32)
    live[0] = row_hot
    live[1] = row_hot * active
    hits[...] = lax.dot_general(
        live[1],
        onehot[...],
        (((1,), (1,)), ((), ())),
        precision=EXACT,
        preferred_element_type=jnp.float32,
    )

    def gather(step, ref):
        flat = jnp.concatenate(
            [ref[comp, 2 + surface, SIDE_ROWS:below] for comp in range(COMPS)], axis=0
        )
        wide = jnp.dot(flat, onehot[...], precision=EXACT, preferred_element_type=jnp.float32)
        for comp in range(COMPS):
            picked = wide[comp * rows : comp * rows + rows] * live[0]
            outgoing[step, comp : comp + 1] = jnp.sum(picked, axis=0, keepdims=True)

    def scatter(step):
        flat = jnp.concatenate(
            [live[1] * received[step, comp : comp + 1] for comp in range(COMPS)], axis=0
        )
        layer[...] = lax.dot_general(
            flat,
            onehot[...],
            (((1,), (1,)), ((), ())),
            precision=EXACT,
            preferred_element_type=jnp.float32,
        )

    gather(0, first)

    load_speed.wait()

    def scale(at, carry):
        speed[at] = STEP_SIZE * speed[at]
        return carry

    lax.fori_loop(0, depth, scale, 0, unroll=8)

    def rim_terms(step, chunk, own):
        place_in_slot = lane & 3
        edge = jnp.where(
            place_in_slot < 2, from_left[step, chunk, own], from_right[step, chunk, own]
        )
        after1, after2, before1, before2 = (
            pltpu.roll(edge, shift, 1) for shift in (cols - 1, cols - 2, 1, 2)
        )
        near = jnp.where(place_in_slot == 1, after1, jnp.where(place_in_slot == 2, before1, 0.0))
        return 16.0 * near - jnp.where(place_in_slot < 2, after2, before2)

    at_rim = (lane < 2) | (lane >= cols - 2)

    def advance(step, chunk):
        source = second if step else first
        base = chunk * CHUNK
        owns = [pl.ds(tile * 8, 8) for tile in range(tiles)]
        rims = [rim_terms(step, chunk, own) for own in owns]
        totals = [jnp.zeros((8, cols), jnp.float32) for _ in owns]
        for comp in range(COMPS):
            block = source[comp, pl.ds(base + 2, CHUNK), pl.ds(SIDE_ROWS, rows)]
            block = block.reshape(CHUNK * rows, cols)
            high = block.astype(jnp.bfloat16)
            low = (block - high.astype(jnp.float32)).astype(jnp.bfloat16)
            width = jnp.dot(
                jnp.concatenate([high, low], axis=1),
                band[...],
                preferred_element_type=jnp.float32,
            )
            for tile, own in enumerate(owns):
                at_row = SIDE_ROWS + tile * 8
                factor = rate[comp, own]
                column = [
                    source[comp, base + at, pl.ds(at_row, 8)] for at in range(CHUNK + 4)
                ]
                for at in range(CHUNK):
                    slot = comp * CHUNK + at
                    here = base + 2 + at
                    value = column[at + 2]
                    up1, up2, down1, down2 = (
                        source[comp, here, pl.ds(at_row + shift, 8)] for shift in (-1, -2, 1, 2)
                    )
                    side = pltpu.roll(rims[tile], (cols - 4 * slot - 2) % cols, 1)
                    start = at * rows + tile * 8
                    sideways = width[start : start + 8] + jnp.where(at_rim, side, 0.0)
                    near = (up1 + down1) + (column[at + 1] + column[at + 3])
                    far = (up2 + down2) + (column[at] + column[at + 4])
                    laplace = (16.0 * near - far) + (sideways - 90.0 * value)
                    flow = speed[base + at, own] * (value - up1)
                    fresh = value + (factor * laplace - flow)
                    if step:
                        result[comp, base + at, own] = fresh
                    else:
                        second[comp, here, pl.ds(at_row, 8)] = fresh
                        totals[tile] = pack(fresh, slot, totals[tile])
        if not step:
            for own, total in zip(owns, totals):
                packed[1, chunk, own] = total

    for index in range(AHEAD):
        pass_on(0, place(index))

    def step_one(index, carry):
        chunk = place(index)

        @pl.when(index + AHEAD < chunks)
        def _():
            pass_on(0, place(index + AHEAD))

        arrive_wid(0, chunk)
        arrive_cast(0, chunk)
        advance(0, chunk)
        send_cast(1, chunk)
        send_wid(1, chunk)
        @pl.when((index == chunks // 2) & bay)
        def _():
            pl.semaphore_wait(word_sem, 1)

        @pl.when(index == chunks // 2)
        def _():
            port_copy(0).start()

        return carry

    for_all(step_one, 0)

    port_copy(0).wait_recv()
    scatter(0)
    inner = pl.ds(SIDE_ROWS + 2, rows - 4)
    for comp in range(COMPS):
        old = second[comp, 2 + surface, inner]
        change = layer[comp * rows + 2 : comp * rows + rows - 2] - hits[2 : rows - 2] * old
        second[comp, 2 + surface, inner] = old + RELAXATION * change
    gather(1, second)
    port_copy(1).start()

    for index in range(AHEAD_AGAIN):
        pass_on(1, place(index))

    def step_two(index, carry):
        chunk = place(index)

        @pl.when(index + AHEAD_AGAIN < chunks)
        def _():
            pass_on(1, place(index + AHEAD_AGAIN))

        arrive_wid(1, chunk)
        arrive_cast(1, chunk)
        advance(1, chunk)

        @pl.when(index == chunks - 4)
        def _():
            port_copy(1).wait_recv()
            scatter(1)
            for comp in range(COMPS):
                old = result[comp, surface]
                change = layer[comp * rows : comp * rows + rows] - hits[...] * old
                result[comp, surface] = old + RELAXATION * change

        return carry

    for_all(step_two, 0)

    for step in range(2):
        sent_cast(step)
        sent_wid(step)
    for step in range(2):
        port_copy(step).wait_send()


def per_device(fields, velocity, liquid_mask, diffusion, port_cell, handoff_count):
    _, comps, depth, rows, cols = fields.shape
    ports = port_cell.shape[-1]
    chunks = depth // CHUNK
    f32 = jnp.float32
    padded = pltpu.VMEM((comps, depth + 4, rows + 2 * SIDE_ROWS, cols), f32)
    strips = pltpu.VMEM((2, chunks, rows, cols), f32)
    dma = pltpu.SemaphoreType.DMA
    return pl.pallas_call(
        kernel,
        out_shape=pltpu.VMEM(fields.shape, f32),
        in_specs=[pl.BlockSpec(memory_space=pltpu.HBM)] * 6,
        out_specs=pl.BlockSpec(memory_space=pltpu.VMEM),
        scratch_shapes=[
            padded,
            padded,
            pltpu.VMEM((depth, rows, cols), f32),
            pltpu.SMEM(liquid_mask.shape, jnp.int32),
            pltpu.SMEM(diffusion.shape, f32),
            pltpu.VMEM(port_cell.shape, jnp.int32),
            pltpu.SMEM(handoff_count.shape, jnp.int32),
            pltpu.VMEM((comps, rows, cols), f32),
            pltpu.VMEM((2 * cols, cols), jnp.bfloat16),
            strips,
            strips,
            strips,
            pltpu.VMEM((cols, ports), f32),
            pltpu.VMEM((2, rows, ports), f32),
            pltpu.VMEM((comps * rows, cols), f32),
            pltpu.VMEM((rows, cols), f32),
            pltpu.VMEM((2, comps, ports), f32),
            pltpu.VMEM((2, comps, ports), f32),
            pltpu.VMEM((2, comps // 2, depth, 2, cols), f32),
            dma((chunks,)),
            dma,
            dma((4,)),
            dma((2, 2)),
            dma((2, 2, chunks)),
            dma((2, 2)),
            dma((2, 2, chunks)),
            dma((2,)),
            dma((2,)),
            pltpu.SemaphoreType.REGULAR,
            dma((2,)),
            dma((2, chunks)),
            dma((2,)),
            dma((2, chunks)),
        ],
        compiler_params=pltpu.CompilerParams(
            collective_id=0, has_side_effects=True, vmem_limit_bytes=54 * 2**20
        ),
        cost_estimate=pl.CostEstimate(
            flops=60 * fields.size, bytes_accessed=9 * 2**20, transcendentals=0
        ),
    )(fields, velocity, liquid_mask, diffusion, port_cell, handoff_count)


def solution(mesh):
    in_specs = (
        P("grp", None, None, "cast", "wid"),
        P("grp", None, "cast", "wid"),
        P("grp", "cast", "wid"),
        P("grp", None),
        P("grp", "cast", "wid", None),
        P("grp", "cast", "wid"),
    )
    out_specs = P("grp", None, None, "cast", "wid")
    return jax.shard_map(
        per_device, mesh=mesh, in_specs=in_specs, out_specs=out_specs, check_vma=False
    )
```
